32 devices in a mesh: col: 16 (over z, y, x), row: 2 (over core).
Axes of the slice: x: 2, y: 2, z: 4, core: 2. Of those that a mesh axis runs over, the one named last changes fastest.
Arguments:
- static_flex: float32 [2048, 8192], P('row', 'col'), may hold values from -6 to 6
- phi_slab: float32 [2048, 1024], P('row', 'col'), may hold values from -6 to 6
- phi_cols: float32 [8192, 1024], P('col', 'row'), may hold values from -6 to 6
- eigenvalues: float32 [1024], P('col'), may hold values from 8 to 128
Outputs:
- residual_flex: float32 [2048, 8192], P('row', 'col')
The draws below stay inside these ranges and needn't reach their ends.
All inputs are finite; a program needn't handle non-finite values.
Results may differ from the reference program's by a relative error of at most 0.00005.
Values sent between devices are 32-bit elements; how exact they have to be, the bound alone decides.
No kernel may reach another device: no remote copies, remote signals or barrier semaphores. Data moves between devices by JAX's collectives and lax.ppermute only.
A program may use at most 64 MiB of HBM per device.

```python
import math
import jax
import jax.numpy as jnp
from jax import lax

MODES = 1024
BOUNDARY = 8192
SLAB = 2048


def level_of(own_key, shape, shards, least, high):
    loudness, own = 1.0, jax.random.fold_in(own_key, 6)
    for dim, shards_of in shards:
        steps = jnp.exp(jax.random.uniform(jax.random.fold_in(own, dim), (shards_of,), jnp.float32, least / len(shards), high / len(shards)))
        loudness = loudness * jnp.repeat(steps, shape[dim] // shards_of).reshape([-1 if axis == dim else 1 for axis in range(len(shape))])
    return loudness


def normal_values(rng, dims, deviation, limit, split=(), kind=jnp.bfloat16):
    gain = level_of(rng, dims, split, -0.22, 0.18) if split else 1.0
    result = jax.random.normal(rng, dims, jnp.float32) * deviation * gain
    return jnp.minimum(jnp.maximum(result, -limit), limit).astype(kind)


def setup_inputs(seed: int = 0) -> dict:
    arg_keys = jax.random.split(jax.random.key(seed), 5)
    static_flex = normal_values(arg_keys[0], (SLAB, BOUNDARY), 1.0, 6.0, ((0, 2), (1, 16)), jnp.float32)
    phi_slab = normal_values(arg_keys[1], (SLAB, MODES), 1.0, 6.0, ((0, 2), (1, 16)), jnp.float32)
    phi_cols = normal_values(arg_keys[2], (BOUNDARY, MODES), 1.0, 6.0, ((0, 16), (1, 2)), jnp.float32)
    eigenvalues = jnp.clip(jnp.exp(math.log(128.0) - 2.7725887 * jax.random.uniform(arg_keys[3], (MODES,), jnp.float32) ** level_of(arg_keys[3], (MODES,), ((0, 16),), -0.2, 0.2)), 8.0, 128.0)
    return {"static_flex": static_flex, "phi_slab": phi_slab, "phi_cols": phi_cols, "eigenvalues": eigenvalues}


def reference(static_flex, phi_slab, phi_cols, eigenvalues):
    scaled = phi_slab / eigenvalues[None, :]
    update = lax.dot_general(scaled, phi_cols, (((1,), (1,)), ((), ())), precision=lax.Precision.HIGHEST, preferred_element_type=jnp.float32)
    return static_flex - update
```

```python
import functools

import jax
import jax.numpy as jnp
from jax import lax
from jax.experimental import pallas as pl
from jax.experimental.pallas import tpu as pltpu
from jax.sharding import PartitionSpec as P

BF16, F32 = jnp.bfloat16, jnp.float32


def moves(layers):
    def perm(target):
        pairs = []
        for z in range(layers):
            for y in range(2):
                for x in range(2):
                    for core in range(2):
                        tz, ty, tx = target(z, y, x, core)
                        pairs.append((((z * 2 + y) * 2 + x) * 2 + core, ((tz * 2 + ty) * 2 + tx) * 2 + core))
        return pairs

    first = perm(lambda z, y, x, core: (z, y, 1 - x) if core == 0 else (z, 1 - y, x))
    second = perm(lambda z, y, x, core: (z, 1 - y, x) if core == 0 else (z, y, 1 - x))
    layer = [perm(lambda z, y, x, core: (z ^ step, y, x)) for step in range(layers)]
    return first, second, layer


def send(value, pairs):
    return lax.ppermute(value, ("col", "row"), pairs)


def after(value, *earlier):
    return lax.optimization_barrier((value, *earlier))[0]


def gather_layers(own):
    first, second, layer = moves(4)
    m = own.shape[0]
    near = send(own, layer[1])
    own_a = send(own, first)
    far = send(own, layer[2])
    own_b = send(own, second)
    pair = send(after(jnp.concatenate([own_a, near]), own_b), second)
    near_a = send(near, first)
    last = send(far, layer[1])
    far_a = send(after(far, near_a), first)
    pair2 = send(after(jnp.concatenate([near_a, far]), pair), second)
    last_a = send(after(last, far_a), first)
    pair3 = send(after(jnp.concatenate([far_a, last]), pair2), second)
    last_d = send(last_a, second)
    return (
        (own, own_a, own_b, pair[:m]),
        (near, near_a, pair[m:], pair2[:m]),
        (far, far_a, pair2[m:], pair3[:m]),
        (last, last_a, pair3[m:], last_d),
    )


def split(value):
    high = value.astype(BF16)
    return high, (value - high.astype(F32)).astype(BF16)


def prepare_kernel(mine_ref, other_ref, high_ref, low_ref, turned):
    col, core = lax.axis_index("col"), lax.axis_index("row")
    layers, depth, _ = high_ref.shape
    m = depth // 4
    half = mine_ref.shape[1] // depth
    z, y, x = col // 4, (col // 2) % 2, col % 2
    ahead = jnp.where(core == 0, 1, 2)
    place = y * 2 + x
    for step in range(layers):
        at = z ^ step
        start = pl.multiple_of((at % half) * depth, depth)

        @pl.when(at // half == core)
        def _():
            turned[...] = mine_ref[:, pl.ds(start, depth)].T

        @pl.when(at // half != core)
        def _():
            turned[...] = other_ref[:, pl.ds(start, depth)].T

        for slot, bits in enumerate((0, ahead, 3 - ahead, 3)):
            block = turned[pl.ds(pl.multiple_of((place ^ bits) * m, m), m), :]
            high, low = split(block)
            high_ref[step, slot * m : (slot + 1) * m, :] = high
            low_ref[step, slot * m : (slot + 1) * m, :] = low


def prepare(mine, other, layers):
    cols, modes = mine.shape
    depth = modes * 2 // layers
    shape = jax.ShapeDtypeStruct((layers, depth, cols), BF16)
    return pl.pallas_call(
        prepare_kernel,
        out_shape=(shape, shape),
        in_specs=[pl.BlockSpec(memory_space=pltpu.VMEM)] * 2,
        out_specs=[pl.BlockSpec(memory_space=pltpu.VMEM)] * 2,
        scratch_shapes=[pltpu.VMEM((depth, cols), F32)],
        compiler_params=pltpu.CompilerParams(vmem_limit_bytes=24 << 20),
        cost_estimate=pl.CostEstimate(flops=0, bytes_accessed=8 * cols * modes * 2, transcendentals=0),
        name="prepare_cols",
    )(mine, other)


def layer_kernel(*refs):
    *unit_refs, high_ref, low_ref, total_ref, out_ref = refs
    left = jnp.concatenate([ref[...] for ref in unit_refs], axis=0).T
    left_high, left_low = split(left)
    dot = functools.partial(jnp.dot, preferred_element_type=F32)
    update = dot(left_high, high_ref[0]) + (dot(left_high, low_ref[0]) + dot(left_low, high_ref[0]))
    out_ref[...] = total_ref[...] - update


def subtract_layer(total, units, high, low, step, tile=256):
    rows, cols = total.shape
    m, depth = units[0].shape[0], high.shape[1]
    cols_spec = pl.BlockSpec((1, depth, cols), lambda i: (step, 0, 0))
    return pl.pallas_call(
        layer_kernel,
        grid=(rows // tile,),
        out_shape=jax.ShapeDtypeStruct((rows, cols), F32),
        in_specs=[pl.BlockSpec((m, tile), lambda i: (0, i))] * 4 + [cols_spec] * 2 + [pl.BlockSpec((tile, cols), lambda i: (i, 0))],
        out_specs=pl.BlockSpec((tile, cols), lambda i: (i, 0)),
        compiler_params=pltpu.CompilerParams(vmem_limit_bytes=24 << 20),
        cost_estimate=pl.CostEstimate(flops=6 * rows * cols * depth, bytes_accessed=8 * rows * cols, transcendentals=0),
        name="subtract_layer",
    )(*units, high, low, total)


def local_by_layers(static_flex, phi_slab, phi_cols, eigenvalues):
    other = lax.ppermute(phi_cols, "row", [(0, 1), (1, 0)])
    scaled = phi_slab.T / eigenvalues[:, None]
    layers = gather_layers(scaled)
    high, low = prepare(phi_cols, other, len(layers))
    total = static_flex
    for step, units in enumerate(layers):
        total = subtract_layer(total, units, high, low, step)
    return total


def local_by_all_gather(static_flex, phi_slab, phi_cols, eigenvalues):
    scaled = phi_slab / eigenvalues[None, :]
    rows_all = lax.all_gather(scaled, "col", axis=1, tiled=True)
    cols_all = lax.all_gather(phi_cols, "row", axis=1, tiled=True)
    update = lax.dot_general(
        rows_all, cols_all, (((1,), (1,)), ((), ())), precision=lax.Precision.HIGHEST, preferred_element_type=F32
    )
    return static_flex - update


def solution(mesh):
    placed = (P("row", "col"), P("row", "col"), P("col", "row"), P("col"))
    four_layers = mesh.shape["col"] == 16 and mesh.shape["row"] == 2
    local = local_by_layers if four_layers else local_by_all_gather
    return jax.shard_map(local, mesh=mesh, in_specs=placed, out_specs=P("row", "col"), check_vma=False)
```

```python
import functools

import jax
import jax.numpy as jnp
from jax import lax
from jax.experimental import pallas as pl
from jax.experimental.pallas import tpu as pltpu
from jax.sharding import PartitionSpec as P

BF16, F32 = jnp.bfloat16, jnp.float32


def moves(layers):
    def perm(target):
        pairs = []
        for z in range(layers):
            for y in range(2):
                for x in range(2):
                    for core in range(2):
                        tz, ty, tx = target(z, y, x, core)
                        pairs.append((((z * 2 + y) * 2 + x) * 2 + core, ((tz * 2 + ty) * 2 + tx) * 2 + core))
        return pairs

    first = perm(lambda z, y, x, core: (z, y, 1 - x) if core == 0 else (z, 1 - y, x))
    second = perm(lambda z, y, x, core: (z, 1 - y, x) if core == 0 else (z, y, 1 - x))
    layer = [perm(lambda z, y, x, core: (z ^ step, y, x)) for step in range(layers)]
    return first, second, layer


def send(value, pairs):
    return lax.ppermute(value, ("col", "row"), pairs)


def together(*values):
    return lax.optimization_barrier(values)


ROUNDS = (
    ((0, 0), (0, 1), (1, 0), (0, 2)),
    ((2, 0), (0, 3), (1, 1), (3, 0)),
    ((2, 1), (2, 2), (1, 2), (2, 3)),
    ((1, 3), (3, 1), (3, 2), (3, 3)),
)


def split(value):
    high = value.astype(BF16)
    return high, (value - high.astype(F32)).astype(BF16)


def prepare_kernel(rounds, mine_ref, other_ref, high_ref, low_ref, turned):
    col, core = lax.axis_index("col"), lax.axis_index("row")
    layers, depth, _ = high_ref.shape
    m = depth // 4
    half = mine_ref.shape[1] // depth
    z, y, x = col // 4, (col // 2) % 2, col % 2
    ahead = jnp.where(core == 0, 1, 2)
    place = y * 2 + x
    for step in range(layers):
        at = z ^ step
        start = pl.multiple_of((at % half) * depth, depth)

        @pl.when(at // half == core)
        def _():
            turned[...] = mine_ref[:, pl.ds(start, depth)].T

        @pl.when(at // half != core)
        def _():
            turned[...] = other_ref[:, pl.ds(start, depth)].T

        bits = (0, ahead, 3 - ahead, 3)
        for i, blocks in enumerate(rounds):
            for slot, (layer, seat) in enumerate(blocks):
                if layer == step:
                    block = turned[pl.ds(pl.multiple_of((place ^ bits[seat]) * m, m), m), :]
                    high, low = split(block)
                    high_ref[i, slot * m : (slot + 1) * m, :] = high
                    low_ref[i, slot * m : (slot + 1) * m, :] = low


def prepare(mine, other, rounds):
    layers = len(rounds)
    cols, modes = mine.shape
    depth = modes * 2 // layers
    shape = jax.ShapeDtypeStruct((layers, depth, cols), BF16)
    return pl.pallas_call(
        functools.partial(prepare_kernel, rounds),
        out_shape=(shape, shape),
        in_specs=[pl.BlockSpec(memory_space=pltpu.VMEM)] * 2,
        out_specs=[pl.BlockSpec(memory_space=pltpu.VMEM)] * 2,
        scratch_shapes=[pltpu.VMEM((depth, cols), F32)],
        compiler_params=pltpu.CompilerParams(vmem_limit_bytes=24 << 20),
        cost_estimate=pl.CostEstimate(flops=0, bytes_accessed=8 * cols * modes * 2, transcendentals=0),
        name="prepare_cols",
    )(mine, other)


def update_tile(unit_refs, high, low, rows):
    left = jnp.concatenate([ref[:, rows] for ref in unit_refs], axis=0).T
    left_high, left_low = split(left)
    dot = functools.partial(jnp.dot, preferred_element_type=F32)
    return dot(left_high, high) + (dot(left_high, low) + dot(left_low, high))


def round_kernel(i, tile, *refs):
    *unit_refs, high_ref, low_ref, total_ref, out_ref = refs
    high, low = high_ref[i], low_ref[i]
    for start in range(0, total_ref.shape[0], tile):
        rows = slice(start, start + tile)
        out_ref[rows, :] = total_ref[rows, :] - update_tile(unit_refs, high, low, rows)


def last_kernel(i, tile, *refs):
    *unit_refs, high_ref, low_ref, total_ref, out_ref, done, sems = refs
    high, low = high_ref[i], low_ref[i]
    copies = []
    for slot, start in enumerate(range(0, total_ref.shape[0], tile)):
        rows = slice(start, start + tile)
        done[rows, :] = total_ref[rows, :] - update_tile(unit_refs, high, low, rows)
        copies.append(pltpu.make_async_copy(done.at[pl.ds(start, tile)], out_ref.at[pl.ds(start, tile)], sems.at[slot]))
        copies[-1].start()
    for copy in copies:
        copy.wait()


def subtract_round(total, units, high, low, i, last=False, tile=256):
    rows, cols = total.shape
    depth = high.shape[1]
    in_vmem = pl.BlockSpec(memory_space=pltpu.VMEM)
    scratch = [pltpu.VMEM((rows, cols), F32), pltpu.SemaphoreType.DMA((rows // tile,))] if last else []
    return pl.pallas_call(
        functools.partial(last_kernel if last else round_kernel, i, tile),
        out_shape=jax.ShapeDtypeStruct((rows, cols), F32),
        in_specs=[in_vmem] * (len(units) + 3),
        out_specs=pl.BlockSpec(memory_space=pl.ANY) if last else in_vmem,
        scratch_shapes=scratch,
        compiler_params=pltpu.CompilerParams(vmem_limit_bytes=24 << 20),
        cost_estimate=pl.CostEstimate(flops=6 * rows * cols * depth, bytes_accessed=8 * rows * cols, transcendentals=0),
        name="subtract_last" if last else "subtract_round",
    )(*units, high, low, total)


def local_by_layers(static_flex, phi_slab, phi_cols, eigenvalues):
    first, second, layer = moves(4)
    other = lax.ppermute(phi_cols, "row", [(0, 1), (1, 0)])
    own = phi_slab.T / eigenvalues[:, None]
    own_a = send(own, first)
    near = send(own, layer[1])
    own_b = send(own, second)
    far = send(own, layer[2])
    high, low = prepare(phi_cols, other, ROUNDS)
    own_d = send(own_a, second)
    near_a = send(near, first)
    far, own_d, own_b, high = together(far, own_d, own_b, high)
    last = send(far, layer[1])
    far_a = send(far, first)
    far, near_a = together(far, near_a)
    far_b = send(far, second)
    near_b = send(own_b, layer[1])
    far_d = send(far_a, second)
    near_d = send(near_a, second)
    total = subtract_round(static_flex, (own, own_a, near, own_b), high, low, 0)
    last, total = together(last, total)
    last_a = send(last, first)
    last_b = send(far_b, layer[1])
    last_d = send(last_a, second)
    total = subtract_round(total, (far, own_d, near_a, last), high, low, 1)
    total = subtract_round(total, (far_a, far_b, near_b, far_d), high, low, 2)
    return subtract_round(total, (near_d, last_a, last_b, last_d), high, low, 3, last=True)


def local_by_all_gather(static_flex, phi_slab, phi_cols, eigenvalues):
    scaled = phi_slab / eigenvalues[None, :]
    rows_all = lax.all_gather(scaled, "col", axis=1, tiled=True)
    cols_all = lax.all_gather(phi_cols, "row", axis=1, tiled=True)
    update = lax.dot_general(
        rows_all, cols_all, (((1,), (1,)), ((), ())), precision=lax.Precision.HIGHEST, preferred_element_type=F32
    )
    return static_flex - update


def solution(mesh):
    placed = (P("row", "col"), P("row", "col"), P("col", "row"), P("col"))
    four_layers = mesh.shape["col"] == 16 and mesh.shape["row"] == 2
    local = local_by_layers if four_layers else local_by_all_gather
    return jax.shard_map(local, mesh=mesh, in_specs=placed, out_specs=P("row", "col"), check_vma=False)
```

```python
import functools

import jax
import jax.numpy as jnp
from jax import lax
from jax.experimental import pallas as pl
from jax.experimental.pallas import tpu as pltpu
from jax.sharding import PartitionSpec as P

BF16, F32 = jnp.bfloat16, jnp.float32


def moves(layers):
    def perm(target):
        pairs = []
        for z in range(layers):
            for y in range(2):
                for x in range(2):
                    for core in range(2):
                        tz, ty, tx = target(z, y, x, core)
                        pairs.append((((z * 2 + y) * 2 + x) * 2 + core, ((tz * 2 + ty) * 2 + tx) * 2 + core))
        return pairs

    first = perm(lambda z, y, x, core: (z, y, 1 - x) if core == 0 else (z, 1 - y, x))
    second = perm(lambda z, y, x, core: (z, 1 - y, x) if core == 0 else (z, y, 1 - x))
    layer = [perm(lambda z, y, x, core: (z ^ step, y, x)) for step in range(layers)]
    return first, second, layer


def send(value, pairs):
    return lax.ppermute(value, ("col", "row"), pairs)


def together(*values):
    return lax.optimization_barrier(values)


ROUNDS = (
    ((0, 0), (0, 1), (1, 0), (0, 2)),
    ((2, 0), (0, 3), (1, 1), (3, 0)),
    ((2, 1), (2, 2), (1, 2), (2, 3), (1, 3), (3, 1)),
    ((3, 2), (3, 3)),
)


def split(value):
    high = value.astype(BF16)
    return high, (value - high.astype(F32)).astype(BF16)


def prepare_kernel(order, mine_ref, other_ref, high_ref, low_ref, turned):
    col, core = lax.axis_index("col"), lax.axis_index("row")
    depth, m = turned.shape[0], turned.shape[0] // 4
    half = mine_ref.shape[1] // depth
    z, y, x = col // 4, (col // 2) % 2, col % 2
    ahead = jnp.where(core == 0, 1, 2)
    turns = (0, ahead, 3 - ahead, 3)
    for step in range(len(order) // 4):
        at = z ^ step
        start = pl.multiple_of((at % half) * depth, depth)

        @pl.when(at // half == core)
        def _():
            turned[...] = mine_ref[:, pl.ds(start, depth)].T

        @pl.when(at // half != core)
        def _():
            turned[...] = other_ref[:, pl.ds(start, depth)].T

        for i, (layer, seat) in enumerate(order):
            if layer == step:
                block = turned[pl.ds(pl.multiple_of(((y * 2 + x) ^ turns[seat]) * m, m), m), :]
                high_ref[i * m : (i + 1) * m, :], low_ref[i * m : (i + 1) * m, :] = split(block)


def prepare(mine, other, rounds):
    order = [block for blocks in rounds for block in blocks]
    cols, modes = mine.shape
    modes *= 2
    shape = jax.ShapeDtypeStruct((modes, cols), BF16)
    return pl.pallas_call(
        functools.partial(prepare_kernel, order),
        out_shape=(shape, shape),
        in_specs=[pl.BlockSpec(memory_space=pltpu.VMEM)] * 2,
        out_specs=[pl.BlockSpec(memory_space=pltpu.VMEM)] * 2,
        scratch_shapes=[pltpu.VMEM((modes * 4 // len(order), cols), F32)],
        compiler_params=pltpu.CompilerParams(vmem_limit_bytes=24 << 20),
        cost_estimate=pl.CostEstimate(flops=0, bytes_accessed=8 * cols * modes, transcendentals=0),
        name="prepare_cols",
    )(mine, other)


def right_side(high_ref, low_ref, modes):
    high, low = high_ref[modes, :], low_ref[modes, :]
    return jnp.concatenate([high, low, high], axis=0)


def update_tile(unit_refs, right, rows):
    left = jnp.concatenate([ref[:, rows] for ref in unit_refs], axis=0).T
    high, low = split(left)
    return jnp.dot(jnp.concatenate([high, high, low], axis=1), right, preferred_element_type=F32)


def round_kernel(modes, tile, *refs):
    *unit_refs, high_ref, low_ref, total_ref, out_ref = refs
    right = right_side(high_ref, low_ref, modes)
    for start in range(0, total_ref.shape[0], tile):
        rows = slice(start, start + tile)
        out_ref[rows, :] = total_ref[rows, :] - update_tile(unit_refs, right, rows)


def last_kernel(modes, tile, *refs):
    *unit_refs, high_ref, low_ref, total_ref, out_ref, done, sems = refs
    right = right_side(high_ref, low_ref, modes)
    copies = []
    for slot, start in enumerate(range(0, total_ref.shape[0], tile)):
        rows = slice(start, start + tile)
        done[rows, :] = total_ref[rows, :] - update_tile(unit_refs, right, rows)
        copies.append(pltpu.make_async_copy(done.at[pl.ds(start, tile)], out_ref.at[pl.ds(start, tile)], sems.at[slot]))
        copies[-1].start()
    for copy in copies:
        copy.wait()


def subtract_round(total, units, high, low, i):
    last = i == len(ROUNDS) - 1
    tile = 128 if last else 256
    rows, cols = total.shape
    m = units[0].shape[0]
    first = m * sum(len(blocks) for blocks in ROUNDS[:i])
    modes = slice(first, first + m * len(units))
    in_vmem = pl.BlockSpec(memory_space=pltpu.VMEM)
    scratch = [pltpu.VMEM((rows, cols), F32), pltpu.SemaphoreType.DMA((rows // tile,))] if last else []
    return pl.pallas_call(
        functools.partial(last_kernel if last else round_kernel, modes, tile),
        out_shape=jax.ShapeDtypeStruct((rows, cols), F32),
        in_specs=[in_vmem] * (len(units) + 3),
        out_specs=pl.BlockSpec(memory_space=pl.ANY) if last else in_vmem,
        scratch_shapes=scratch,
        compiler_params=pltpu.CompilerParams(vmem_limit_bytes=24 << 20),
        cost_estimate=pl.CostEstimate(flops=6 * rows * cols * m * len(units), bytes_accessed=8 * rows * cols, transcendentals=0),
        name="subtract_last" if last else "subtract_round",
    )(*units, high, low, total)


def local_by_layers(static_flex, phi_slab, phi_cols, eigenvalues):
    first, second, layer = moves(4)
    other = lax.ppermute(phi_cols, "row", [(0, 1), (1, 0)])
    own = phi_slab.T / eigenvalues[:, None]
    own_a = send(own, first)
    near = send(own, layer[1])
    own_b = send(own, second)
    far = send(own, layer[2])
    high, low = prepare(phi_cols, other, ROUNDS)
    own_d = send(own_a, second)
    near_a = send(near, first)
    far, own_b, high = together(far, own_b, high)
    last = send(far, layer[1])
    far_a = send(far, first)
    own_a, far, own_d, own_b, near_a = together(own_a, far, own_d, own_b, near_a)
    far_b = send(far, second)
    near_b = send(own_b, layer[1])
    far_d = send(far_a, second)
    near_d = send(near_a, second)
    total = subtract_round(static_flex, (own, own_a, near, own_b), high, low, 0)
    last, total = together(last, total)
    last_a = send(last, first)
    last_b = send(far_b, layer[1])
    last_d = send(last_a, second)
    total = subtract_round(total, (far, own_d, near_a, last), high, low, 1)
    total = subtract_round(total, (far_a, far_b, near_b, far_d, near_d, last_a), high, low, 2)
    return subtract_round(total, (last_b, last_d), high, low, 3)


def local_by_all_gather(static_flex, phi_slab, phi_cols, eigenvalues):
    scaled = phi_slab / eigenvalues[None, :]
    rows_all = lax.all_gather(scaled, "col", axis=1, tiled=True)
    cols_all = lax.all_gather(phi_cols, "row", axis=1, tiled=True)
    update = lax.dot_general(
        rows_all, cols_all, (((1,), (1,)), ((), ())), precision=lax.Precision.HIGHEST, preferred_element_type=F32
    )
    return static_flex - update


def solution(mesh):
    placed = (P("row", "col"), P("row", "col"), P("col", "row"), P("col"))
    four_layers = mesh.shape["col"] == 16 and mesh.shape["row"] == 2
    local = local_by_layers if four_layers else local_by_all_gather
    return jax.shard_map(local, mesh=mesh, in_specs=placed, out_specs=P("row", "col"), check_vma=False)
```

```python
import functools

import jax
import jax.numpy as jnp
from jax import lax
from jax.experimental import pallas as pl
from jax.experimental.pallas import tpu as pltpu
from jax.sharding import PartitionSpec as P

BF16, F32 = jnp.bfloat16, jnp.float32


def moves(layers):
    def perm(target):
        pairs = []
        for z in range(layers):
            for y in range(2):
                for x in range(2):
                    for core in range(2):
                        tz, ty, tx = target(z, y, x, core)
                        pairs.append((((z * 2 + y) * 2 + x) * 2 + core, ((tz * 2 + ty) * 2 + tx) * 2 + core))
        return pairs

    first = perm(lambda z, y, x, core: (z, y, 1 - x) if core == 0 else (z, 1 - y, x))
    second = perm(lambda z, y, x, core: (z, 1 - y, x) if core == 0 else (z, y, 1 - x))
    layer = [perm(lambda z, y, x, core: (z ^ step, y, x)) for step in range(layers)]
    return first, second, layer


def send(value, pairs):
    return lax.ppermute(value, ("col", "row"), pairs)


def together(*values):
    return lax.optimization_barrier(values)


ROUNDS = (
    ((0, 0), (0, 1), (1, 0), (0, 2)),
    ((2, 0), (0, 3), (1, 1), (3, 0)),
    ((2, 1), (2, 2), (1, 2), (2, 3), (1, 3), (3, 1)),
    ((3, 2), (3, 3)),
)


def split(value):
    high = value.astype(BF16)
    return high, (value - high.astype(F32)).astype(BF16)


def prepare_kernel(order, mine_ref, other_ref, high_ref, low_ref, turned):
    col, core = lax.axis_index("col"), lax.axis_index("row")
    depth, m = turned.shape[0], turned.shape[0] // 4
    half = mine_ref.shape[1] // depth
    z, y, x = col // 4, (col // 2) % 2, col % 2
    ahead = jnp.where(core == 0, 1, 2)
    turns = (0, ahead, 3 - ahead, 3)
    for step in range(len(order) // 4):
        at = z ^ step
        start = pl.multiple_of((at % half) * depth, depth)

        @pl.when(at // half == core)
        def _():
            turned[...] = mine_ref[:, pl.ds(start, depth)].T

        @pl.when(at // half != core)
        def _():
            turned[...] = other_ref[:, pl.ds(start, depth)].T

        for i, (layer, seat) in enumerate(order):
            if layer == step:
                block = turned[pl.ds(pl.multiple_of(((y * 2 + x) ^ turns[seat]) * m, m), m), :]
                high_ref[i * m : (i + 1) * m, :], low_ref[i * m : (i + 1) * m, :] = split(block)


def prepare(mine, other, rounds):
    order = [block for blocks in rounds for block in blocks]
    cols, modes = mine.shape
    modes *= 2
    shape = jax.ShapeDtypeStruct((modes, cols), BF16)
    return pl.pallas_call(
        functools.partial(prepare_kernel, order),
        out_shape=(shape, shape),
        in_specs=[pl.BlockSpec(memory_space=pltpu.VMEM)] * 2,
        out_specs=[pl.BlockSpec(memory_space=pltpu.VMEM)] * 2,
        scratch_shapes=[pltpu.VMEM((modes * 4 // len(order), cols), F32)],
        compiler_params=pltpu.CompilerParams(vmem_limit_bytes=24 << 20),
        cost_estimate=pl.CostEstimate(flops=0, bytes_accessed=8 * cols * modes, transcendentals=0),
        name="prepare_cols",
    )(mine, other)


def right_side(high_ref, low_ref, modes):
    high, low = high_ref[modes, :], low_ref[modes, :]
    return jnp.concatenate([high, low, high], axis=0)


def update_tile(unit_refs, right, rows):
    left = jnp.concatenate([ref[:, rows] for ref in unit_refs], axis=0).T
    high, low = split(left)
    return jnp.dot(jnp.concatenate([high, high, low], axis=1), right, preferred_element_type=F32)


def round_kernel(modes, tile, *refs):
    *unit_refs, high_ref, low_ref, total_ref, out_ref = refs
    right = right_side(high_ref, low_ref, modes)
    for start in range(0, total_ref.shape[0], tile):
        rows = slice(start, start + tile)
        out_ref[rows, :] = total_ref[rows, :] - update_tile(unit_refs, right, rows)


def last_kernel(modes, tile, *refs):
    *unit_refs, high_ref, low_ref, total_ref, out_ref, done, sems = refs
    right = right_side(high_ref, low_ref, modes)
    copies = []
    for slot, start in enumerate(range(0, total_ref.shape[0], tile)):
        rows = slice(start, start + tile)
        done[rows, :] = total_ref[rows, :] - update_tile(unit_refs, right, rows)
        copies.append(pltpu.make_async_copy(done.at[pl.ds(start, tile)], out_ref.at[pl.ds(start, tile)], sems.at[slot]))
        copies[-1].start()
    for copy in copies:
        copy.wait()


def subtract_round(total, units, high, low, i):
    last = i == len(ROUNDS) - 1
    tile = 128 if last else 256
    rows, cols = total.shape
    m = units[0].shape[0]
    first = m * sum(len(blocks) for blocks in ROUNDS[:i])
    modes = slice(first, first + m * len(units))
    in_vmem = pl.BlockSpec(memory_space=pltpu.VMEM)
    scratch = [pltpu.VMEM((rows, cols), F32), pltpu.SemaphoreType.DMA((rows // tile,))] if last else []
    return pl.pallas_call(
        functools.partial(last_kernel if last else round_kernel, modes, tile),
        out_shape=jax.ShapeDtypeStruct((rows, cols), F32),
        in_specs=[in_vmem] * (len(units) + 3),
        out_specs=pl.BlockSpec(memory_space=pl.ANY) if last else in_vmem,
        scratch_shapes=scratch,
        compiler_params=pltpu.CompilerParams(vmem_limit_bytes=24 << 20),
        cost_estimate=pl.CostEstimate(flops=6 * rows * cols * m * len(units), bytes_accessed=8 * rows * cols, transcendentals=0),
        name="subtract_last" if last else "subtract_round",
    )(*units, high, low, total)


def local_by_layers(static_flex, phi_slab, phi_cols, eigenvalues):
    first, second, layer = moves(4)
    other = lax.ppermute(phi_cols, "row", [(0, 1), (1, 0)])
    own = phi_slab.T / eigenvalues[:, None]
    own_a = send(own, first)
    near = send(own, layer[1])
    own_b = send(own, second)
    far = send(own, layer[2])
    high, low = prepare(phi_cols, other, ROUNDS)
    own_d = send(own_a, second)
    near_a = send(near, first)
    far, own_b, high = together(far, own_b, high)
    own_a, near, own_d = together(own_a, near, own_d)
    last = send(far, layer[1])
    far_a = send(far, first)
    own_a, far, own_d, own_b, near_a = together(own_a, far, own_d, own_b, near_a)
    far_b = send(far, second)
    near_b = send(own_b, layer[1])
    total = subtract_round(static_flex, (own, own_a, near, own_b), high, low, 0)
    far_d = send(far_a, second)
    near_d = send(near_a, second)
    last_a = send(last, first)
    last_b = send(far_b, layer[1])
    last_a, total = together(last_a, total)
    total = subtract_round(total, (far, own_d, near_a, last), high, low, 1)
    last_d = send(last_a, second)
    total = subtract_round(total, (far_a, far_b, near_b, far_d, near_d, last_a), high, low, 2)
    return subtract_round(total, (last_b, last_d), high, low, 3)


def local_by_all_gather(static_flex, phi_slab, phi_cols, eigenvalues):
    scaled = phi_slab / eigenvalues[None, :]
    rows_all = lax.all_gather(scaled, "col", axis=1, tiled=True)
    cols_all = lax.all_gather(phi_cols, "row", axis=1, tiled=True)
    update = lax.dot_general(
        rows_all, cols_all, (((1,), (1,)), ((), ())), precision=lax.Precision.HIGHEST, preferred_element_type=F32
    )
    return static_flex - update


def solution(mesh):
    placed = (P("row", "col"), P("row", "col"), P("col", "row"), P("col"))
    four_layers = mesh.shape["col"] == 16 and mesh.shape["row"] == 2
    local = local_by_layers if four_layers else local_by_all_gather
    return jax.shard_map(local, mesh=mesh, in_specs=placed, out_specs=P("row", "col"), check_vma=False)
```

```python
import functools

import jax
import jax.numpy as jnp
from jax import lax
from jax.experimental import pallas as pl
from jax.experimental.pallas import tpu as pltpu
from jax.sharding import PartitionSpec as P

BF16, F32 = jnp.bfloat16, jnp.float32


def moves(layers):
    def perm(target):
        pairs = []
        for z in range(layers):
            for y in range(2):
                for x in range(2):
                    for core in range(2):
                        tz, ty, tx = target(z, y, x, core)
                        pairs.append((((z * 2 + y) * 2 + x) * 2 + core, ((tz * 2 + ty) * 2 + tx) * 2 + core))
        return pairs

    first = perm(lambda z, y, x, core: (z, y, 1 - x) if core == 0 else (z, 1 - y, x))
    second = perm(lambda z, y, x, core: (z, 1 - y, x) if core == 0 else (z, y, 1 - x))
    layer = [perm(lambda z, y, x, core: (z ^ step, y, x)) for step in range(layers)]
    return first, second, layer


def send(value, pairs):
    return lax.ppermute(value, ("col", "row"), pairs)


def together(*values):
    return lax.optimization_barrier(values)


ROUNDS = (
    ((0, 0), (0, 1), (1, 0), (0, 2)),
    ((2, 0), (0, 3), (1, 1), (3, 0), (2, 1), (2, 2)),
    ((1, 2), (2, 3), (1, 3), (3, 1)),
    ((3, 2), (3, 3)),
)


def split(value):
    high = value.astype(BF16)
    return high, (value - high.astype(F32)).astype(BF16)


def prepare_kernel(order, mine_ref, other_ref, high_ref, low_ref, turned):
    col, core = lax.axis_index("col"), lax.axis_index("row")
    depth, m = turned.shape[0], turned.shape[0] // 4
    half = mine_ref.shape[1] // depth
    z, y, x = col // 4, (col // 2) % 2, col % 2
    ahead = jnp.where(core == 0, 1, 2)
    turns = (0, ahead, 3 - ahead, 3)
    for step in range(len(order) // 4):
        at = z ^ step
        start = pl.multiple_of((at % half) * depth, depth)

        @pl.when(at // half == core)
        def _():
            turned[...] = mine_ref[:, pl.ds(start, depth)].T

        @pl.when(at // half != core)
        def _():
            turned[...] = other_ref[:, pl.ds(start, depth)].T

        for i, (layer, seat) in enumerate(order):
            if layer == step:
                block = turned[pl.ds(pl.multiple_of(((y * 2 + x) ^ turns[seat]) * m, m), m), :]
                high_ref[i * m : (i + 1) * m, :], low_ref[i * m : (i + 1) * m, :] = split(block)


def prepare(mine, other, rounds):
    order = [block for blocks in rounds for block in blocks]
    cols, modes = mine.shape
    modes *= 2
    shape = jax.ShapeDtypeStruct((modes, cols), BF16)
    return pl.pallas_call(
        functools.partial(prepare_kernel, order),
        out_shape=(shape, shape),
        in_specs=[pl.BlockSpec(memory_space=pltpu.VMEM)] * 2,
        out_specs=[pl.BlockSpec(memory_space=pltpu.VMEM)] * 2,
        scratch_shapes=[pltpu.VMEM((modes * 4 // len(order), cols), F32)],
        compiler_params=pltpu.CompilerParams(vmem_limit_bytes=24 << 20),
        cost_estimate=pl.CostEstimate(flops=0, bytes_accessed=8 * cols * modes, transcendentals=0),
        name="prepare_cols",
    )(mine, other)


def right_side(high_ref, low_ref, modes):
    high, low = high_ref[modes, :], low_ref[modes, :]
    return jnp.concatenate([high, low, high], axis=0)


def update_tile(unit_refs, right, rows):
    left = jnp.concatenate([ref[:, rows] for ref in unit_refs], axis=0).T
    high, low = split(left)
    return jnp.dot(jnp.concatenate([high, high, low], axis=1), right, preferred_element_type=F32)


def round_kernel(modes, tile, *refs):
    *unit_refs, high_ref, low_ref, total_ref, out_ref = refs
    right = right_side(high_ref, low_ref, modes)
    for start in range(0, total_ref.shape[0], tile):
        rows = slice(start, start + tile)
        out_ref[rows, :] = total_ref[rows, :] - update_tile(unit_refs, right, rows)


def last_kernel(modes, tile, *refs):
    *unit_refs, high_ref, low_ref, total_ref, out_ref, done, sems = refs
    right = right_side(high_ref, low_ref, modes)
    copies = []
    for slot, start in enumerate(range(0, total_ref.shape[0], tile)):
        rows = slice(start, start + tile)
        done[rows, :] = total_ref[rows, :] - update_tile(unit_refs, right, rows)
        copies.append(pltpu.make_async_copy(done.at[pl.ds(start, tile)], out_ref.at[pl.ds(start, tile)], sems.at[slot]))
        copies[-1].start()
    for copy in copies:
        copy.wait()


def subtract_round(total, units, high, low, i):
    last = i == len(ROUNDS) - 1
    tile = 128 if last else 256
    rows, cols = total.shape
    m = units[0].shape[0]
    first = m * sum(len(blocks) for blocks in ROUNDS[:i])
    modes = slice(first, first + m * len(units))
    in_vmem = pl.BlockSpec(memory_space=pltpu.VMEM)
    scratch = [pltpu.VMEM((rows, cols), F32), pltpu.SemaphoreType.DMA((rows // tile,))] if last else []
    return pl.pallas_call(
        functools.partial(last_kernel if last else round_kernel, modes, tile),
        out_shape=jax.ShapeDtypeStruct((rows, cols), F32),
        in_specs=[in_vmem] * (len(units) + 3),
        out_specs=pl.BlockSpec(memory_space=pl.ANY) if last else in_vmem,
        scratch_shapes=scratch,
        compiler_params=pltpu.CompilerParams(vmem_limit_bytes=24 << 20),
        cost_estimate=pl.CostEstimate(flops=6 * rows * cols * m * len(units), bytes_accessed=8 * rows * cols, transcendentals=0),
        name="subtract_last" if last else "subtract_round",
    )(*units, high, low, total)


def local_by_layers(static_flex, phi_slab, phi_cols, eigenvalues):
    first, second, layer = moves(4)
    other = lax.ppermute(phi_cols, "row", [(0, 1), (1, 0)])
    own = phi_slab.T / eigenvalues[:, None]
    own_a = send(own, first)
    near = send(own, layer[1])
    own_b = send(own, second)
    far = send(own, layer[2])
    high, low = prepare(phi_cols, other, ROUNDS)
    own_d = send(own_a, second)
    near_a = send(near, first)
    far, own_b, high = together(far, own_b, high)
    own_a, near, own_d = together(own_a, near, own_d)
    last = send(far, layer[1])
    far_a = send(far, first)
    own_a, far, own_d, own_b, near_a = together(own_a, far, own_d, own_b, near_a)
    far_b = send(far, second)
    near_b = send(own_b, layer[1])
    total = subtract_round(static_flex, (own, own_a, near, own_b), high, low, 0)
    far_d = send(far_a, second)
    near_d = send(near_a, second)
    last_a = send(last, first)
    last_b = send(far_b, layer[1])
    last_a, total = together(last_a, total)
    total = subtract_round(total, (far, own_d, near_a, last, far_a, far_b), high, low, 1)
    last_d = send(last_a, second)
    total = subtract_round(total, (near_b, far_d, near_d, last_a), high, low, 2)
    return subtract_round(total, (last_b, last_d), high, low, 3)


def local_by_all_gather(static_flex, phi_slab, phi_cols, eigenvalues):
    scaled = phi_slab / eigenvalues[None, :]
    rows_all = lax.all_gather(scaled, "col", axis=1, tiled=True)
    cols_all = lax.all_gather(phi_cols, "row", axis=1, tiled=True)
    update = lax.dot_general(
        rows_all, cols_all, (((1,), (1,)), ((), ())), precision=lax.Precision.HIGHEST, preferred_element_type=F32
    )
    return static_flex - update


def solution(mesh):
    placed = (P("row", "col"), P("row", "col"), P("col", "row"), P("col"))
    four_layers = mesh.shape["col"] == 16 and mesh.shape["row"] == 2
    local = local_by_layers if four_layers else local_by_all_gather
    return jax.shard_map(local, mesh=mesh, in_specs=placed, out_specs=P("row", "col"), check_vma=False)
```

```python
import functools

import jax
import jax.numpy as jnp
from jax import lax
from jax.experimental import pallas as pl
from jax.experimental.pallas import tpu as pltpu
from jax.sharding import PartitionSpec as P

BF16, F32 = jnp.bfloat16, jnp.float32


def moves(layers):
    def perm(target):
        pairs = []
        for z in range(layers):
            for y in range(2):
                for x in range(2):
                    for core in range(2):
                        tz, ty, tx = target(z, y, x, core)
                        pairs.append((((z * 2 + y) * 2 + x) * 2 + core, ((tz * 2 + ty) * 2 + tx) * 2 + core))
        return pairs

    first = perm(lambda z, y, x, core: (z, y, 1 - x) if core == 0 else (z, 1 - y, x))
    second = perm(lambda z, y, x, core: (z, 1 - y, x) if core == 0 else (z, y, 1 - x))
    layer = [perm(lambda z, y, x, core: (z ^ step, y, x)) for step in range(layers)]
    return first, second, layer


def send(value, pairs):
    return lax.ppermute(value, ("col", "row"), pairs)


def together(*values):
    return lax.optimization_barrier(values)


ROUNDS = (
    ((0, 0), (0, 1), (1, 0), (0, 2)),
    ((2, 0), (0, 3), (1, 1), (3, 0)),
    ((2, 1), (2, 2), (1, 2), (2, 3), (1, 3), (3, 1)),
    ((3, 2), (3, 3)),
)


def split(value):
    high = value.astype(BF16)
    return high, (value - high.astype(F32)).astype(BF16)


def prepare_kernel(order, mine_ref, other_ref, high_ref, low_ref, turned):
    col, core = lax.axis_index("col"), lax.axis_index("row")
    depth, m = turned.shape[0], turned.shape[0] // 4
    half = mine_ref.shape[1] // depth
    z, y, x = col // 4, (col // 2) % 2, col % 2
    ahead = jnp.where(core == 0, 1, 2)
    turns = (0, ahead, 3 - ahead, 3)
    for step in range(len(order) // 4):
        at = z ^ step
        start = pl.multiple_of((at % half) * depth, depth)

        @pl.when(at // half == core)
        def _():
            turned[...] = mine_ref[:, pl.ds(start, depth)].T

        @pl.when(at // half != core)
        def _():
            turned[...] = other_ref[:, pl.ds(start, depth)].T

        for i, (layer, seat) in enumerate(order):
            if layer == step:
                block = turned[pl.ds(pl.multiple_of(((y * 2 + x) ^ turns[seat]) * m, m), m), :]
                high_ref[i * m : (i + 1) * m, :], low_ref[i * m : (i + 1) * m, :] = split(block)


def prepare(mine, other, rounds):
    order = [block for blocks in rounds for block in blocks]
    cols, modes = mine.shape
    modes *= 2
    shape = jax.ShapeDtypeStruct((modes, cols), BF16)
    return pl.pallas_call(
        functools.partial(prepare_kernel, order),
        out_shape=(shape, shape),
        in_specs=[pl.BlockSpec(memory_space=pltpu.VMEM)] * 2,
        out_specs=[pl.BlockSpec(memory_space=pltpu.VMEM)] * 2,
        scratch_shapes=[pltpu.VMEM((modes * 4 // len(order), cols), F32)],
        compiler_params=pltpu.CompilerParams(vmem_limit_bytes=24 << 20),
        cost_estimate=pl.CostEstimate(flops=0, bytes_accessed=8 * cols * modes, transcendentals=0),
        name="prepare_cols",
    )(mine, other)


def right_side(high_ref, low_ref, modes):
    high, low = high_ref[modes, :], low_ref[modes, :]
    return jnp.concatenate([high, low, high], axis=0)


def update_tile(unit_refs, right, rows):
    left = jnp.concatenate([ref[:, rows] for ref in unit_refs], axis=0).T
    high, low = split(left)
    return jnp.dot(jnp.concatenate([high, high, low], axis=1), right, preferred_element_type=F32)


def round_kernel(modes, tile, *refs):
    *unit_refs, high_ref, low_ref, total_ref, out_ref = refs
    right = right_side(high_ref, low_ref, modes)
    for start in range(0, total_ref.shape[0], tile):
        rows = slice(start, start + tile)
        out_ref[rows, :] = total_ref[rows, :] - update_tile(unit_refs, right, rows)


def last_kernel(modes, tile, *refs):
    *unit_refs, high_ref, low_ref, total_ref, out_ref, done, sems = refs
    right = right_side(high_ref, low_ref, modes)
    copies = []
    for slot, start in enumerate(range(0, total_ref.shape[0], tile)):
        rows = slice(start, start + tile)
        done[rows, :] = total_ref[rows, :] - update_tile(unit_refs, right, rows)
        copies.append(pltpu.make_async_copy(done.at[pl.ds(start, tile)], out_ref.at[pl.ds(start, tile)], sems.at[slot]))
        copies[-1].start()
    for copy in copies:
        copy.wait()


def subtract_round(total, units, high, low, i):
    last = i == len(ROUNDS) - 1
    tile = 128 if last else 256
    rows, cols = total.shape
    m = units[0].shape[0]
    first = m * sum(len(blocks) for blocks in ROUNDS[:i])
    modes = slice(first, first + m * len(units))
    in_vmem = pl.BlockSpec(memory_space=pltpu.VMEM)
    scratch = [pltpu.VMEM((rows, cols), F32), pltpu.SemaphoreType.DMA((rows // tile,))] if last else []
    return pl.pallas_call(
        functools.partial(last_kernel if last else round_kernel, modes, tile),
        out_shape=jax.ShapeDtypeStruct((rows, cols), F32),
        in_specs=[in_vmem] * (len(units) + 3),
        out_specs=pl.BlockSpec(memory_space=pl.ANY) if last else in_vmem,
        scratch_shapes=scratch,
        compiler_params=pltpu.CompilerParams(vmem_limit_bytes=24 << 20),
        cost_estimate=pl.CostEstimate(flops=6 * rows * cols * m * len(units), bytes_accessed=8 * rows * cols, transcendentals=0),
        name="subtract_last" if last else "subtract_round",
    )(*units, high, low, total)


def local_by_layers(static_flex, phi_slab, phi_cols, eigenvalues):
    first, second, layer = moves(4)
    other = lax.ppermute(phi_cols, "row", [(0, 1), (1, 0)])
    own = phi_slab.T / eigenvalues[:, None]
    own_a = send(own, first)
    near = send(own, layer[1])
    own_b = send(own, second)
    far = send(own, layer[2])
    high, low = prepare(phi_cols, other, ROUNDS)
    own_d = send(own_a, second)
    near_a = send(near, first)
    far, own_b, high = together(far, own_b, high)
    own_a, near, own_d = together(own_a, near, own_d)
    last = send(far, layer[1])
    far_a = send(far, first)
    own_a, far, own_d, own_b, near_a = together(own_a, far, own_d, own_b, near_a)
    far_b = send(far, second)
    near_b = send(own_b, layer[1])
    total = subtract_round(static_flex, (own, own_a, near, own_b), high, low, 0)
    far_d = send(far_a, second)
    near_d = send(near_a, second)
    last_a = send(last, first)
    last_b = send(far_b, layer[1])
    total = subtract_round(total, (far, own_d, near_a, last), high, low, 1)
    last_d = send(last_a, second)
    total = subtract_round(total, (far_a, far_b, near_b, far_d, near_d, last_a), high, low, 2)
    return subtract_round(total, (last_b, last_d), high, low, 3)


def local_by_all_gather(static_flex, phi_slab, phi_cols, eigenvalues):
    scaled = phi_slab / eigenvalues[None, :]
    rows_all = lax.all_gather(scaled, "col", axis=1, tiled=True)
    cols_all = lax.all_gather(phi_cols, "row", axis=1, tiled=True)
    update = lax.dot_general(
        rows_all, cols_all, (((1,), (1,)), ((), ())), precision=lax.Precision.HIGHEST, preferred_element_type=F32
    )
    return static_flex - update


def solution(mesh):
    placed = (P("row", "col"), P("row", "col"), P("col", "row"), P("col"))
    four_layers = mesh.shape["col"] == 16 and mesh.shape["row"] == 2
    local = local_by_layers if four_layers else local_by_all_gather
    return jax.shard_map(local, mesh=mesh, in_specs=placed, out_specs=P("row", "col"), check_vma=False)
```
